32 devices in a mesh: row: 8 (over z, core), col: 4 (over y, x).
Axes of the slice: x: 2, y: 2, z: 4, core: 2. Of those that a mesh axis runs over, the one named last changes fastest.
Arguments:
- hidden_pre: bfloat16 [512, 16384], P('col', 'row'), may hold values from -6 to 6
- weight_blocks: bfloat16 [8, 4, 8, 256, 256], P('row', 'col'), may hold values from -0.09375 to 0.09375
- block_rows: int32 [8, 4, 8], P('row', 'col'), may hold values from 0 to 63, as said below
- block_cols: int32 [8, 4, 8], P('row', 'col'), may hold values from 0 to 31, as said below
- block_counts: int32 [8, 4], P('row', 'col'), may hold values from 2 to 8, as said below
- out_grad: bfloat16 [512, 8192], P('row', 'col'), may hold values from -6 to 6
Outputs:
- projected: bfloat16 [512, 8192], P('row', 'col')
- grad_hidden: bfloat16 [512, 16384], P('col', 'row')
- grad_blocks: float32 [8, 4, 8, 256, 256], P('row', 'col')
The draws below stay inside these ranges and needn't reach their ends.
Inputs may be any that keep to these rules, and one draw needn't show every extreme that they name: `block_rows`: owner (r, c) holds only blocks of block-rows r * 8 to (r + 1) * 8 - 1 and block-columns c * 8 to (c + 1) * 8 - 1; the 8 slots of one owner name 8 different blocks. `block_cols`: same owner ranges as block_rows. `block_counts`: some owner holds exactly 8 live blocks and some owner exactly 2.
All inputs are finite; a program needn't handle non-finite values.
Results may differ from the reference program's by a relative error of at most 0.0051.
Values may be sent and summed in bfloat16 or wider, within the bound.
A program may use at most 128 MiB of HBM per device.

```python
import jax
import jax.numpy as jnp
from jax import lax

D = 8192
FF = 16384
BS = 256
CAP = 8
TOKENS = 512
ROW_OWNERS = 8
COL_OWNERS = 4
ROW_BLOCKS = 8
COL_BLOCKS = 8
TILE = 64


def tile_order(key):
    score = jax.random.randint(jax.random.fold_in(key, 11), (ROW_OWNERS, COL_OWNERS, TILE), 0, 4096)
    score = score * TILE + jnp.arange(TILE, dtype=jnp.int32)[None, None, :]
    owner_r = jnp.arange(ROW_OWNERS, dtype=jnp.int32)[:, None, None]
    owner_c = jnp.arange(COL_OWNERS, dtype=jnp.int32)[None, :, None]
    spot = jnp.arange(TILE, dtype=jnp.int32)[None, None, :]
    first = (owner_r == 0) & (owner_c == 0) & (spot == 0)
    final = (owner_r == ROW_OWNERS - 1) & (owner_c == COL_OWNERS - 1) & (spot == TILE - 1)
    score = jnp.where(first | final, -1, score)
    return jnp.argsort(score, axis=-1)[:, :, :CAP].astype(jnp.int32)


def draw_block_rows(key, part):
    order = tile_order(key)
    owner = jnp.arange(ROW_OWNERS, dtype=jnp.int32)[:, None, None]
    return (owner * ROW_BLOCKS + order // COL_BLOCKS).astype(jnp.int32)


def draw_block_cols(key, part):
    order = tile_order(key)
    owner = jnp.arange(COL_OWNERS, dtype=jnp.int32)[None, :, None]
    return (owner * COL_BLOCKS + order % COL_BLOCKS).astype(jnp.int32)


def draw_block_counts(key, part):
    total = ROW_OWNERS * COL_OWNERS
    counts = jax.random.randint(key, (total,), 2, CAP + 1)
    chosen = jax.random.randint(jax.random.fold_in(key, 5), (), 0, total)
    places = jnp.arange(total, dtype=jnp.int32)
    counts = jnp.where(places == chosen, CAP, counts)
    counts = jnp.where(places == (chosen + 1) % total, 2, counts)
    return counts.reshape(ROW_OWNERS, COL_OWNERS).astype(jnp.int32)


def steps_of(own_key, dims, cuts, low, high):
    def one(position, blocks):
        steps = jax.random.uniform(jax.random.fold_in(jax.random.fold_in(own_key, 6), position), (blocks,), jnp.float32, low / len(cuts), high / len(cuts))
        return jnp.repeat(jnp.exp(steps), dims[position] // blocks).reshape((-1,) + (1,) * (len(dims) - position - 1))

    loudness = one(*cuts[0])
    for cut in cuts[1:]:
        loudness = loudness * one(*cut)
    return loudness


def normal_values(rng, dims, scale, most, cuts=(), kind=jnp.bfloat16):
    array = scale * jax.random.normal(rng, dims, jnp.float32)
    if cuts:
        array = array * steps_of(rng, dims, cuts, -0.22, 0.18)
    return jnp.clip(array, -most, most).astype(kind)


def setup_inputs(seed: int = 0) -> dict:
    keys = jax.random.split(jax.random.key(seed), 7)
    return {
        "hidden_pre": normal_values(keys[0], (TOKENS, FF), 1.0, 6.0, ((0, 4), (1, 8))),
        "weight_blocks": normal_values(keys[1], (ROW_OWNERS, COL_OWNERS, CAP, BS, BS), (FF // 4) ** -0.5, 0.09375, ((0, 8), (1, 4))),
        "block_rows": draw_block_rows(jax.random.fold_in(keys[6], 71), 0),
        "block_cols": draw_block_cols(jax.random.fold_in(keys[6], 71), 0),
        "block_counts": draw_block_counts(jax.random.fold_in(keys[6], 71), 0),
        "out_grad": normal_values(keys[5], (TOKENS, D), 1.0, 6.0, ((0, 8), (1, 4))),
    }


def reference(hidden_pre, weight_blocks, block_rows, block_cols, block_counts, out_grad):
    hidden_f = hidden_pre.astype(jnp.float32)
    act = jax.nn.silu(hidden_f).astype(jnp.bfloat16)
    slots = jnp.arange(CAP, dtype=jnp.int32)
    live = (slots[None, None, :] < block_counts[:, :, None]).reshape(-1)
    flat_w = weight_blocks.reshape(-1, BS, BS)
    flat_rows = block_rows.reshape(-1).astype(jnp.int32)
    flat_cols = block_cols.reshape(-1).astype(jnp.int32)

    def step(carry, item):
        out_acc, back_acc = carry
        w_blk, brow, bcol, alive = item

        def active(unused):
            a_blk = lax.dynamic_slice_in_dim(act, brow * BS, BS, 1)
            g_blk = lax.dynamic_slice_in_dim(out_grad, bcol * BS, BS, 1)
            old_out = lax.dynamic_slice_in_dim(out_acc, bcol * BS, BS, 1)
            new_out = lax.dynamic_update_slice_in_dim(out_acc, old_out + jnp.dot(a_blk, w_blk, preferred_element_type=jnp.float32), bcol * BS, 1)
            old_back = lax.dynamic_slice_in_dim(back_acc, brow * BS, BS, 1)
            new_back = lax.dynamic_update_slice_in_dim(back_acc, old_back + jnp.dot(g_blk, w_blk.T, preferred_element_type=jnp.float32), brow * BS, 1)
            grad = jnp.dot(a_blk.T, g_blk, preferred_element_type=jnp.float32)
            return (new_out, new_back), grad

        def skipped(unused):
            return (out_acc, back_acc), jnp.zeros((BS, BS), jnp.float32)

        return lax.cond(alive, active, skipped, None)

    start = (jnp.zeros((TOKENS, D), jnp.float32), jnp.zeros((TOKENS, FF), jnp.float32))
    (out_acc, back_acc), grads = lax.scan(step, start, (flat_w, flat_rows, flat_cols, live))
    projected = out_acc.astype(jnp.bfloat16)
    sig = jax.nn.sigmoid(hidden_f)
    grad_hidden = (back_acc * (sig * (1.0 + hidden_f * (1.0 - sig)))).astype(jnp.bfloat16)
    grad_blocks = grads.reshape(ROW_OWNERS, COL_OWNERS, CAP, BS, BS)
    return projected, grad_hidden, grad_blocks
```

```python
import functools

import jax
import jax.numpy as jnp
from jax import lax
from jax.experimental import pallas as pl
from jax.experimental.pallas import tpu as pltpu
from jax.sharding import PartitionSpec as P

MESH = pl.DeviceIdType.MESH
F32 = jnp.float32
BF16 = jnp.bfloat16


def silu_rounded(values):
    return jax.nn.silu(values.astype(jnp.float32)).astype(jnp.bfloat16)


def plain_on_device(hidden_pre, weight_blocks, block_rows, block_cols, block_counts, out_grad):
    width = weight_blocks.shape[-1]
    slot_count = weight_blocks.shape[2]
    row_span = hidden_pre.shape[1] // width
    col_span = out_grad.shape[1] // width
    row_base = lax.axis_index("row") * row_span
    row_local = block_rows[0, 0] - row_base
    col_local = block_cols[0, 0] - lax.axis_index("col") * col_span
    alive = jnp.arange(slot_count, dtype=jnp.int32) < block_counts[0, 0]
    w_live = jnp.where(
        alive[:, None, None], weight_blocks[0, 0], jnp.zeros_like(weight_blocks[0, 0])
    )
    row_pick = (row_local[:, None] == jnp.arange(row_span, dtype=jnp.int32)[None, :]).astype(
        jnp.float32
    )
    col_pick = (col_local[:, None] == jnp.arange(col_span, dtype=jnp.int32)[None, :]).astype(
        jnp.float32
    )
    grad_full = lax.all_gather(out_grad, "row", axis=0, tiled=True)
    act_rows = silu_rounded(lax.all_gather(hidden_pre, "col", axis=0, tiled=True))
    count = act_rows.shape[0]
    a_stack = jnp.take(act_rows.reshape(count, row_span, width), row_local, axis=1)
    prod = jnp.einsum("nkp,kpq->nkq", a_stack, w_live, preferred_element_type=jnp.float32)
    placed = jnp.einsum("nkq,kc->ncq", prod, col_pick, precision=lax.Precision.HIGHEST)
    partial_value = placed.reshape(count, col_span * width)
    grad_rows = grad_full
    act_rows = silu_rounded(lax.all_gather(hidden_pre, "col", axis=0, tiled=True))
    count = act_rows.shape[0]
    a_stack = jnp.take(act_rows.reshape(count, row_span, width), row_local, axis=1)
    g_stack = jnp.take(grad_rows.reshape(count, col_span, width), col_local, axis=1)
    weight_grad = jnp.einsum("nkp,nkq->kpq", a_stack, g_stack, preferred_element_type=jnp.float32)
    projected = lax.psum_scatter(partial_value, "row", scatter_dimension=0, tiled=True).astype(
        jnp.bfloat16
    )
    count = hidden_pre.shape[0] * lax.axis_size("col")
    grad_rows = grad_full
    g_stack = jnp.take(grad_rows.reshape(count, col_span, width), col_local, axis=1)
    back = jnp.einsum("nkq,kpq->nkp", g_stack, w_live, preferred_element_type=jnp.float32)
    placed = jnp.einsum("nkp,kr->nrp", back, row_pick, precision=lax.Precision.HIGHEST)
    back_act = lax.psum_scatter(
        placed.reshape(count, row_span * width), "col", scatter_dimension=0, tiled=True
    )
    hidden_f = hidden_pre.astype(jnp.float32)
    sig = jax.nn.sigmoid(hidden_f)
    grad_hidden = (back_act * (sig * (1.0 + hidden_f * (1.0 - sig)))).astype(jnp.bfloat16)
    grad_blocks = jnp.where(alive[:, None, None], weight_grad, jnp.zeros_like(weight_grad))
    return (projected, grad_hidden, grad_blocks[None, None])


def fused_kernel(
    hidden_ref, w_ref, rows_ref, cols_ref, count_ref, grad_ref,
    proj_ref, gh_ref, gb_ref,
    act_all, g_all, stage, acc, dsilu, bk, rx, ry, r2a, r2b, s2a, s2b,
    pj, ps, psum, rz, prev_c, last_c, prev_r, last_r,
    a_send, a_recv, zg_send, zg_recv, zf_send, zf_recv, ps_send, ps_recv,
    rz_send, rz_recv, b_send, b_recv,
):
    slots, width = w_ref.shape[0], w_ref.shape[1]
    nb = act_all.shape[0]
    nc = g_all.shape[0]
    half = nb // 2
    group = hidden_ref.shape[0]
    shard = grad_ref.shape[0]
    row, col = lax.axis_index("row"), lax.axis_index("col")
    z, core = lax.div(row, 2), lax.rem(row, 2)
    y, x = lax.div(col, 2), lax.rem(col, 2)
    x_peer = {"col": y * 2 + 1 - x}
    y_peer = {"col": (1 - y) * 2 + x}
    sibling = {"row": z * 2 + 1 - core}
    group_of = [
        y * 2 + x,
        y * 2 + 1 - x,
        (1 - y) * 2 + x,
        (1 - y) * 2 + 1 - x,
    ]

    def chip(offset):
        return lax.rem(z + offset, 4)

    def z_peer(offset):
        return {"row": chip(offset) * 2 + core}

    def remote(src, dst, send, recv, to):
        return pltpu.make_async_remote_copy(
            src_ref=src, dst_ref=dst, send_sem=send, recv_sem=recv,
            device_id=to, device_id_type=MESH,
        )

    barrier = pltpu.get_barrier_semaphore()
    for peer in (sibling, x_peer, y_peer, z_peer(1), z_peer(2), z_peer(3)):
        pl.semaphore_signal(barrier, inc=1, device_id=peer, device_id_type=MESH)

    mine = pl.ds(pl.multiple_of(col * group, group), group)
    own_rows = pl.ds(pl.multiple_of(row * shard, shard), shard)
    for b in range(nb):
        v = hidden_ref[:, b * width:(b + 1) * width].astype(F32)
        act_all[b, mine, :] = (v * (1.0 / (1.0 + jnp.exp(-v)))).astype(BF16)
    for b in range(nc):
        g_all[b, own_rows, :] = grad_ref[:, b * width:(b + 1) * width]
    pl.semaphore_wait(barrier, 6)

    low, high = pl.ds(0, half), pl.ds(half, half)

    def act_view(part, j):
        return act_all.at[part, pl.ds(pl.multiple_of(j * group, group), group), :]

    def g_view(r):
        return g_all.at[:, pl.ds(pl.multiple_of(r * shard, shard), shard), :]

    def act_copy(i, part, j, to):
        return remote(act_view(part, j), act_view(part, j), a_send.at[i], a_recv.at[i], to)

    a_out = [
        act_copy(0, low, group_of[0], x_peer),
        act_copy(1, high, group_of[0], y_peer),
        act_copy(2, high, group_of[0], x_peer),
        act_copy(3, low, group_of[0], y_peer),
        act_copy(4, low, group_of[1], y_peer),
        act_copy(5, high, group_of[2], x_peer),
    ]
    a_in = [
        act_copy(0, low, group_of[1], x_peer),
        act_copy(1, high, group_of[2], y_peer),
        act_copy(2, high, group_of[1], x_peer),
        act_copy(3, low, group_of[2], y_peer),
        act_copy(4, low, group_of[3], y_peer),
        act_copy(5, high, group_of[3], x_peer),
    ]
    zg_out = [None] + [
        remote(g_view(row), g_view(row), zg_send.at[o], zg_recv.at[o], z_peer(o))
        for o in (1, 2, 3)
    ]
    zg_in, zf_out, zf_in = [], [], []
    for o in range(4):
        got = chip(4 - o) * 2 + core
        other = chip(4 - o) * 2 + 1 - core
        zg_in.append(remote(g_view(got), g_view(got), zg_send.at[o], zg_recv.at[o], z_peer(o)))
        zf_out.append(remote(g_view(got), g_view(got), zf_send.at[o], zf_recv.at[o], sibling))
        zf_in.append(remote(g_view(other), g_view(other), zf_send.at[o], zf_recv.at[o], sibling))

    for i in range(4):
        a_out[i].start()
    zf_out[0].start()
    for o in (1, 2, 3):
        zg_out[o].start()

    count = count_ref[0]
    row_of = [lax.rem(rows_ref[k], nb) for k in range(slots)]
    col_of = [lax.rem(cols_ref[k], nc) for k in range(slots)]
    for of, prev, last, span in ((col_of, prev_c, last_c, nc), (row_of, prev_r, last_r, nb)):
        for k in range(slots):
            p = jnp.int32(slots)
            for j in range(k):
                p = jnp.where(of[j] == of[k], j, p)
            prev[k] = p
        for b in range(span):
            p = jnp.int32(slots)
            for k in range(slots):
                p = jnp.where((of[k] == b) & (k < count), k, p)
            last[b] = p
    acc[slots] = jnp.zeros(acc.shape[1:], F32)

    def chain(src, slot_of, span, prev, dims):
        def step(k, carry):
            a = stage[lax.rem(slot_of[k], span)]
            prod = lax.dot_general(a, w_ref[k], (dims, ((), ())), preferred_element_type=F32)
            acc[k] = prod + acc[prev[k]]
            return carry
        stage[...] = src
        lax.fori_loop(0, slots, step, 0, unroll=True)

    def rows_of(j):
        return pl.ds(pl.multiple_of(j * group, group), group)

    ps_out = []

    def forward(d):
        chain(act_all[:, rows_of(group_of[d]), :], rows_ref, nb, prev_c, ((1,), (0,)))

        def put(b, carry):
            pj[d, b] = acc[last_c[b]].astype(BF16)
            return carry
        lax.fori_loop(0, nc, put, 0, unroll=True)
        away = pl.ds(pl.multiple_of((1 - core) * shard, shard), shard)
        ps_out.append(remote(pj.at[d, :, away, :], ps.at[d], ps_send.at[d], ps_recv.at[d], sibling))
        ps_out[d].start()

    def rz_copy(d):
        j = group_of[d]
        return remote(
            psum.at[d], rz.at[lax.rem(j - z + 4, 4)], rz_send.at[d],
            rz_recv.at[lax.rem(j - z + 4, 4)], {"row": j * 2 + core},
        )

    def finish_forward(d):
        ps_out[d].wait_recv()
        keep = pl.ds(pl.multiple_of(core * shard, shard), shard)
        psum[d] = (pj[d, :, keep, :].astype(F32) + ps[d].astype(F32)).astype(BF16)

        @pl.when(group_of[d] != z)
        def _():
            rz_copy(d).start()

    def backward(o):
        j = chip(4 - o)
        chain(g_all[:, rows_of(j), :], cols_ref, nc, prev_r, ((1,), (1,)))
        d = lax.rem(lax.div(j, 2) + y, 2) * 2 + lax.rem(lax.rem(j, 2) + x, 2)

        def put(b, carry):
            bk[d, b] = acc[last_r[b]].astype(BF16)
            return carry
        lax.fori_loop(0, nb, put, 0, unroll=True)

    forward(0)
    zf_in[0].wait_recv()
    backward(0)
    finish_forward(0)
    a_in[0].wait_recv()
    a_out[4].start()
    a_in[1].wait_recv()
    a_out[5].start()
    for b in range(nb):
        v = hidden_ref[:, b * width:(b + 1) * width].astype(F32)
        s = 1.0 / (1.0 + jnp.exp(-v))
        dsilu[b] = s * (1.0 + v * (1.0 - s))
    a_in[2].wait_recv()
    forward(1)
    a_in[3].wait_recv()
    forward(2)
    finish_forward(1)
    finish_forward(2)
    for o in (1, 2, 3):
        zg_in[o].wait_recv()
        zf_out[o].start()
    for o in (1, 2, 3):
        zf_in[o].wait_recv()
        backward(o)

    b_out = [
        remote(bk.at[3, low], rx.at[1], b_send.at[0], b_recv.at[0], x_peer),
        remote(bk.at[3, high], ry.at[1], b_send.at[1], b_recv.at[1], y_peer),
        remote(bk.at[1, low], rx.at[0], b_send.at[2], b_recv.at[2], x_peer),
        remote(bk.at[2, high], ry.at[0], b_send.at[3], b_recv.at[3], y_peer),
        remote(s2a, r2a, b_send.at[4], b_recv.at[4], y_peer),
        remote(s2b, r2b, b_send.at[5], b_recv.at[5], x_peer),
    ]
    for i in range(4):
        b_out[i].start()
    a_in[4].wait_recv()
    a_in[5].wait_recv()
    forward(3)
    finish_forward(3)
    b_out[0].wait_recv()
    s2a[...] = (bk[2, low].astype(F32) + rx[1].astype(F32)).astype(BF16)
    b_out[4].start()
    b_out[1].wait_recv()
    s2b[...] = (bk[1, high].astype(F32) + ry[1].astype(F32)).astype(BF16)
    b_out[5].start()

    def weight_grad(k, carry):
        a = act_all[lax.rem(rows_ref[k], nb)]
        g = g_all[lax.rem(cols_ref[k], nc)]
        value = lax.dot_general(a, g, (((0,), (0,)), ((), ())), preferred_element_type=F32)
        gb_ref[k] = jnp.where(k < count, value, jnp.zeros_like(value))
        return carry
    lax.fori_loop(0, slots, weight_grad, 0, unroll=True)

    for o in (1, 2, 3):
        remote(rz.at[o], rz.at[o], rz_send.at[o], rz_recv.at[o], z_peer(o)).wait_recv()
    d = lax.rem(lax.div(z, 2) + y, 2) * 2 + lax.rem(lax.rem(z, 2) + x, 2)
    for b in range(nc):
        total = psum[d, b].astype(F32)
        for o in (1, 2, 3):
            total = total + rz[o, b].astype(F32)
        proj_ref[:, b * width:(b + 1) * width] = total.astype(BF16)

    b_out[2].wait_recv()
    b_out[4].wait_recv()
    for b in range(half):
        total = bk[0, b].astype(F32) + rx[0, b].astype(F32) + r2a[b].astype(F32)
        gh_ref[:, b * width:(b + 1) * width] = (total * dsilu[b]).astype(BF16)
    b_out[3].wait_recv()
    b_out[5].wait_recv()
    for b in range(half):
        total = bk[0, half + b].astype(F32) + ry[0, b].astype(F32) + r2b[b].astype(F32)
        gh_ref[:, (half + b) * width:(half + b + 1) * width] = (total * dsilu[half + b]).astype(BF16)

    for copy in a_out + zg_out[1:] + zf_out + ps_out + b_out:
        copy.wait_send()
    for d in range(4):
        @pl.when(group_of[d] != z)
        def _():
            rz_copy(d).wait_send()


def fused_on_device(hidden_pre, weight_blocks, block_rows, block_cols, block_counts, out_grad):
    slots, width = weight_blocks.shape[2], weight_blocks.shape[3]
    group, shard = hidden_pre.shape[0], out_grad.shape[0]
    nb, nc = hidden_pre.shape[1] // width, out_grad.shape[1] // width
    tokens = group * lax.axis_size("col")
    half = nb // 2
    vmem = pl.BlockSpec(memory_space=pltpu.VMEM)
    smem = pl.BlockSpec(memory_space=pltpu.SMEM)
    dma = pltpu.SemaphoreType.DMA
    out = pl.pallas_call(
        fused_kernel,
        out_shape=(
            jax.ShapeDtypeStruct(out_grad.shape, BF16),
            jax.ShapeDtypeStruct(hidden_pre.shape, BF16),
            jax.ShapeDtypeStruct((slots, width, width), F32),
        ),
        in_specs=[vmem, vmem, smem, smem, smem, vmem],
        out_specs=(vmem, vmem, vmem),
        scratch_shapes=[
            pltpu.VMEM((nb, tokens, width), BF16),
            pltpu.VMEM((nc, tokens, width), BF16),
            pltpu.VMEM((max(nb, nc), group, width), BF16),
            pltpu.VMEM((slots + 1, group, width), F32),
            pltpu.VMEM((nb, group, width), F32),
            pltpu.VMEM((4, nb, group, width), BF16),
            pltpu.VMEM((2, half, group, width), BF16),
            pltpu.VMEM((2, half, group, width), BF16),
            pltpu.VMEM((half, group, width), BF16),
            pltpu.VMEM((half, group, width), BF16),
            pltpu.VMEM((half, group, width), BF16),
            pltpu.VMEM((half, group, width), BF16),
            pltpu.VMEM((4, nc, group, width), BF16),
            pltpu.VMEM((4, nc, shard, width), BF16),
            pltpu.VMEM((4, nc, shard, width), BF16),
            pltpu.VMEM((4, nc, shard, width), BF16),
            pltpu.SMEM((slots,), jnp.int32),
            pltpu.SMEM((nc,), jnp.int32),
            pltpu.SMEM((slots,), jnp.int32),
            pltpu.SMEM((nb,), jnp.int32),
            dma((6,)), dma((6,)), dma((4,)), dma((4,)), dma((4,)), dma((4,)),
            dma((4,)), dma((4,)), dma((4,)), dma((4,)), dma((6,)), dma((6,)),
        ],
        compiler_params=pltpu.CompilerParams(
            collective_id=0, has_side_effects=True, vmem_limit_bytes=44 * 1024 * 1024
        ),
    )(
        hidden_pre, weight_blocks[0, 0], block_rows[0, 0], block_cols[0, 0],
        block_counts[0], out_grad,
    )
    return out[0], out[1], out[2][None, None]


def on_device(hidden_pre, weight_blocks, block_rows, block_cols, block_counts, out_grad):
    fits = (
        lax.axis_size("row") == 8
        and lax.axis_size("col") == 4
        and hidden_pre.shape[0] == 2 * out_grad.shape[0]
        and hidden_pre.shape[1] == out_grad.shape[1]
    )
    body = fused_on_device if fits else plain_on_device
    return body(hidden_pre, weight_blocks, block_rows, block_cols, block_counts, out_grad)


def solution(mesh):
    placed = (
        P("col", "row"),
        P("row", "col", None, None, None),
        P("row", "col", None),
        P("row", "col", None),
        P("row", "col"),
        P("row", "col"),
    )
    return jax.shard_map(
        on_device,
        mesh=mesh,
        in_specs=placed,
        out_specs=(P("row", "col"), P("col", "row"), P("row", "col", None, None, None)),
        check_vma=False,
    )
```

```python
import functools

import jax
import jax.numpy as jnp
from jax import lax
from jax.experimental import pallas as pl
from jax.experimental.pallas import tpu as pltpu
from jax.sharding import PartitionSpec as P

MESH = pl.DeviceIdType.MESH
F32 = jnp.float32
BF16 = jnp.bfloat16


def silu_rounded(values):
    return jax.nn.silu(values.astype(jnp.float32)).astype(jnp.bfloat16)


def pick_blocks(blocks, which):
    return jnp.stack(
        [
            lax.dynamic_index_in_dim(blocks, which[k], axis=1, keepdims=False)
            for k in range(which.shape[0])
        ],
        axis=1,
    )


def plain_on_device(hidden_pre, weight_blocks, block_rows, block_cols, block_counts, out_grad):
    width = weight_blocks.shape[-1]
    slot_count = weight_blocks.shape[2]
    row_span = hidden_pre.shape[1] // width
    col_span = out_grad.shape[1] // width
    row_base = lax.axis_index("row") * row_span
    row_local = block_rows[0, 0] - row_base
    col_local = block_cols[0, 0] - lax.axis_index("col") * col_span
    alive = jnp.arange(slot_count, dtype=jnp.int32) < block_counts[0, 0]
    w_live = jnp.where(
        alive[:, None, None], weight_blocks[0, 0], jnp.zeros_like(weight_blocks[0, 0])
    )
    row_pick = (row_local[:, None] == jnp.arange(row_span, dtype=jnp.int32)[None, :]).astype(
        jnp.float32
    )
    col_pick = (col_local[:, None] == jnp.arange(col_span, dtype=jnp.int32)[None, :]).astype(
        jnp.float32
    )
    grad_full = lax.all_gather(out_grad, "row", axis=0, tiled=True)
    act_rows = silu_rounded(lax.all_gather(hidden_pre, "col", axis=0, tiled=True))
    count = act_rows.shape[0]
    a_stack = pick_blocks(act_rows.reshape(count, row_span, width), row_local)
    prod = jnp.einsum("nkp,kpq->nkq", a_stack, w_live, preferred_element_type=jnp.float32)
    placed = jnp.einsum("nkq,kc->ncq", prod, col_pick, precision=lax.Precision.HIGHEST)
    partial_value = placed.reshape(count, col_span * width)
    grad_rows = grad_full
    act_rows = silu_rounded(lax.all_gather(hidden_pre, "col", axis=0, tiled=True))
    count = act_rows.shape[0]
    a_stack = pick_blocks(act_rows.reshape(count, row_span, width), row_local)
    g_stack = pick_blocks(grad_rows.reshape(count, col_span, width), col_local)
    weight_grad = jnp.einsum("nkp,nkq->kpq", a_stack, g_stack, preferred_element_type=jnp.float32)
    projected = lax.psum_scatter(partial_value, "row", scatter_dimension=0, tiled=True).astype(
        jnp.bfloat16
    )
    count = hidden_pre.shape[0] * lax.axis_size("col")
    grad_rows = grad_full
    g_stack = pick_blocks(grad_rows.reshape(count, col_span, width), col_local)
    back = jnp.einsum("nkq,kpq->nkp", g_stack, w_live, preferred_element_type=jnp.float32)
    placed = jnp.einsum("nkp,kr->nrp", back, row_pick, precision=lax.Precision.HIGHEST)
    back_act = lax.psum_scatter(
        placed.reshape(count, row_span * width), "col", scatter_dimension=0, tiled=True
    )
    hidden_f = hidden_pre.astype(jnp.float32)
    sig = jax.nn.sigmoid(hidden_f)
    grad_hidden = (back_act * (sig * (1.0 + hidden_f * (1.0 - sig)))).astype(jnp.bfloat16)
    grad_blocks = jnp.where(alive[:, None, None], weight_grad, jnp.zeros_like(weight_grad))
    return (projected, grad_hidden, grad_blocks[None, None])


def fused_kernel(
    hidden_hbm, w_hbm, rows_hbm, cols_hbm, count_hbm, grad_hbm,
    proj_ref, gh_ref, gb_ref,
    hidden_ref, w_buf, rows_buf, cols_buf, count_buf, grad_ref, in_sem,
    act_all, g_all, stage, acc, dsilu, bk, rx, ry, r2a, r2b, s2a, s2b,
    pj, ps, psum, ch, prev_c, last_c, prev_r, last_r,
    a_send, a_recv, zg_send, zg_recv, zf_send, zf_recv, ps_send, ps_recv,
    c_send, c_recv, b_send, b_recv,
):
    w_ref, rows_ref, cols_ref = w_buf.at[0, 0], rows_buf.at[0, 0], cols_buf.at[0, 0]
    slots, width = w_buf.shape[2], w_buf.shape[3]
    nb = act_all.shape[0]
    nc = g_all.shape[0]
    half = nb // 2
    split = half * width
    group = hidden_ref.shape[0]
    shard = grad_ref.shape[0]
    row, col = lax.axis_index("row"), lax.axis_index("col")
    z, core = lax.div(row, 2), lax.rem(row, 2)
    y, x = lax.div(col, 2), lax.rem(col, 2)
    x_peer = {"col": y * 2 + 1 - x}
    y_peer = {"col": (1 - y) * 2 + x}
    sibling = {"row": z * 2 + 1 - core}
    group_of = [
        y * 2 + x,
        y * 2 + 1 - x,
        (1 - y) * 2 + x,
        (1 - y) * 2 + 1 - x,
    ]

    def chip(offset):
        return lax.rem(z + offset, 4)

    def z_peer(offset):
        return {"row": chip(offset) * 2 + core}

    def remote(src, dst, send, recv, to):
        return pltpu.make_async_remote_copy(
            src_ref=src, dst_ref=dst, send_sem=send, recv_sem=recv,
            device_id=to, device_id_type=MESH,
        )

    ins = [
        pltpu.make_async_copy(src, dst, in_sem.at[i])
        for i, (src, dst) in enumerate((
            (hidden_hbm.at[:, pl.ds(0, split)], hidden_ref.at[:, pl.ds(0, split)]),
            (hidden_hbm.at[:, pl.ds(split, split)], hidden_ref.at[:, pl.ds(split, split)]),
            (grad_hbm, grad_ref),
            (rows_hbm, rows_buf),
            (cols_hbm, cols_buf),
            (count_hbm, count_buf),
            (w_hbm, w_buf),
        ))
    ]
    for copy in ins:
        copy.start()
    barrier = pltpu.get_barrier_semaphore()
    for peer in (sibling, x_peer, y_peer, z_peer(1), z_peer(2), z_peer(3)):
        pl.semaphore_signal(barrier, inc=1, device_id=peer, device_id_type=MESH)

    mine = pl.ds(pl.multiple_of(col * group, group), group)
    own_rows = pl.ds(pl.multiple_of(row * shard, shard), shard)

    def activate(blocks):
        for b in blocks:
            v = hidden_ref[:, b * width:(b + 1) * width].astype(F32)
            act_all[b, mine, :] = (v * (1.0 / (1.0 + jnp.exp(-v)))).astype(BF16)

    low, high = pl.ds(0, half), pl.ds(half, half)

    def act_view(part, j):
        return act_all.at[part, pl.ds(pl.multiple_of(j * group, group), group), :]

    def g_view(r):
        return g_all.at[:, pl.ds(pl.multiple_of(r * shard, shard), shard), :]

    def act_copy(i, part, j, to):
        return remote(act_view(part, j), act_view(part, j), a_send.at[i], a_recv.at[i], to)

    a_out = [
        act_copy(0, low, group_of[0], x_peer),
        act_copy(1, high, group_of[0], y_peer),
        act_copy(2, high, group_of[0], x_peer),
        act_copy(3, low, group_of[0], y_peer),
        act_copy(4, low, group_of[1], y_peer),
        act_copy(5, high, group_of[2], x_peer),
    ]
    a_in = [
        act_copy(0, low, group_of[1], x_peer),
        act_copy(1, high, group_of[2], y_peer),
        act_copy(2, high, group_of[1], x_peer),
        act_copy(3, low, group_of[2], y_peer),
        act_copy(4, low, group_of[3], y_peer),
        act_copy(5, high, group_of[3], x_peer),
    ]
    zg_out = [None] + [
        remote(g_view(row), g_view(row), zg_send.at[o], zg_recv.at[o], z_peer(o))
        for o in (1, 2, 3)
    ]
    zg_in, zf_out, zf_in = [], [], []
    for o in range(4):
        got = chip(4 - o) * 2 + core
        other = chip(4 - o) * 2 + 1 - core
        zg_in.append(remote(g_view(got), g_view(got), zg_send.at[o], zg_recv.at[o], z_peer(o)))
        zf_out.append(remote(g_view(got), g_view(got), zf_send.at[o], zf_recv.at[o], sibling))
        zf_in.append(remote(g_view(other), g_view(other), zf_send.at[o], zf_recv.at[o], sibling))

    ins[0].wait()
    activate(range(half))
    pl.semaphore_wait(barrier, 6)
    a_out[0].start()
    a_out[3].start()
    ins[2].wait()
    for b in range(nc):
        g_all[b, own_rows, :] = grad_ref[:, b * width:(b + 1) * width]
    zf_out[0].start()
    for o in (1, 2, 3):
        zg_out[o].start()
    ins[1].wait()
    activate(range(half, nb))
    a_out[1].start()
    a_out[2].start()
    for copy in ins[3:]:
        copy.wait()

    count = count_buf[0, 0]
    row_of = [lax.rem(rows_ref[k], nb) for k in range(slots)]
    col_of = [lax.rem(cols_ref[k], nc) for k in range(slots)]
    for of, prev, last, span in ((col_of, prev_c, last_c, nc), (row_of, prev_r, last_r, nb)):
        for k in range(slots):
            p = jnp.int32(slots)
            for j in range(k):
                p = jnp.where(of[j] == of[k], j, p)
            prev[k] = p
        for b in range(span):
            p = jnp.int32(slots)
            for k in range(slots):
                p = jnp.where((of[k] == b) & (k < count), k, p)
            last[b] = p
    acc[slots] = jnp.zeros(acc.shape[1:], F32)

    def chain(src, slot_of, span, prev, dims):
        def step(k, carry):
            a = stage[lax.rem(slot_of[k], span)]
            prod = lax.dot_general(a, w_ref[k], (dims, ((), ())), preferred_element_type=F32)
            acc[k] = prod + acc[prev[k]]
            return carry
        stage[...] = src
        lax.fori_loop(0, slots, step, 0, unroll=True)

    def rows_of(j):
        return pl.ds(pl.multiple_of(j * group, group), group)

    ps_out = []

    def forward(d):
        chain(act_all[:, rows_of(group_of[d]), :], rows_ref, nb, prev_c, ((1,), (0,)))

        def put(b, carry):
            pj[d, b] = acc[last_c[b]].astype(BF16)
            return carry
        lax.fori_loop(0, nc, put, 0, unroll=True)
        away = pl.ds(pl.multiple_of((1 - core) * shard, shard), shard)
        ps_out.append(remote(pj.at[d, :, away, :], ps.at[d], ps_send.at[d], ps_recv.at[d], sibling))
        ps_out[d].start()

    def advance(d, hop):
        j = group_of[d]
        way = jnp.where(j > z, 0, 1)
        place = jnp.where(j > z, z, 3 - z)
        onward = {"row": (z + 1 - 2 * way) * 2 + core}

        @pl.when((j != z) & (place == hop))
        def _():
            keep = pl.ds(pl.multiple_of(core * shard, shard), shard)
            total = pj[d, :, keep, :].astype(F32) + ps[d].astype(F32)
            copy = remote(
                psum.at[d], ch.at[way, d], c_send.at[d], c_recv.at[way, d], onward
            )
            if hop > 0:
                copy.wait_recv()
                total = total + ch[way, d].astype(F32)
            psum[d] = total.astype(BF16)
            copy.start()

    def pair_sum(d):
        ps_out[d].wait_recv()
        advance(d, 0)

    def backward(o):
        j = chip(4 - o)
        chain(g_all[:, rows_of(j), :], cols_ref, nc, prev_r, ((1,), (1,)))
        d = lax.rem(lax.div(j, 2) + y, 2) * 2 + lax.rem(lax.rem(j, 2) + x, 2)

        def put(b, carry):
            bk[d, b] = acc[last_r[b]].astype(BF16)
            return carry
        lax.fori_loop(0, nb, put, 0, unroll=True)

    forward(0)
    zf_in[0].wait_recv()
    backward(0)
    pair_sum(0)
    a_in[0].wait_recv()
    a_out[4].start()
    a_in[1].wait_recv()
    a_out[5].start()
    for b in range(nb):
        v = hidden_ref[:, b * width:(b + 1) * width].astype(F32)
        s = 1.0 / (1.0 + jnp.exp(-v))
        dsilu[b] = s * (1.0 + v * (1.0 - s))
    a_in[2].wait_recv()
    forward(1)
    a_in[3].wait_recv()
    forward(2)
    pair_sum(1)
    pair_sum(2)
    advance(0, 1)
    for o in (1, 2, 3):
        zg_in[o].wait_recv()
        zf_out[o].start()
    for o in (1, 2, 3):
        zf_in[o].wait_recv()
        backward(o)

    b_out = [
        remote(bk.at[3, low], rx.at[1], b_send.at[0], b_recv.at[0], x_peer),
        remote(bk.at[3, high], ry.at[1], b_send.at[1], b_recv.at[1], y_peer),
        remote(bk.at[1, low], rx.at[0], b_send.at[2], b_recv.at[2], x_peer),
        remote(bk.at[2, high], ry.at[0], b_send.at[3], b_recv.at[3], y_peer),
        remote(s2a, r2a, b_send.at[4], b_recv.at[4], y_peer),
        remote(s2b, r2b, b_send.at[5], b_recv.at[5], x_peer),
    ]
    for i in range(4):
        b_out[i].start()
    a_in[4].wait_recv()
    a_in[5].wait_recv()
    forward(3)
    advance(0, 2)
    advance(1, 1)
    advance(2, 1)
    pair_sum(3)
    advance(1, 2)
    advance(2, 2)
    advance(3, 1)
    b_out[0].wait_recv()
    s2a[...] = (bk[2, low].astype(F32) + rx[1].astype(F32)).astype(BF16)
    b_out[4].start()
    b_out[1].wait_recv()
    s2b[...] = (bk[1, high].astype(F32) + ry[1].astype(F32)).astype(BF16)
    b_out[5].start()

    def weight_grad(k, carry):
        a = act_all[lax.rem(rows_ref[k], nb)]
        g = g_all[lax.rem(cols_ref[k], nc)]
        value = lax.dot_general(a, g, (((0,), (0,)), ((), ())), preferred_element_type=F32)
        gb_ref[k] = jnp.where(k < count, value, jnp.zeros_like(value))
        return carry
    lax.fori_loop(0, slots, weight_grad, 0, unroll=True)

    advance(3, 2)
    d = lax.rem(lax.div(z, 2) + y, 2) * 2 + lax.rem(lax.rem(z, 2) + x, 2)

    def arrived(way, edge):
        @pl.when(z == edge)
        def _():
            ch[way, d] = jnp.zeros(ch.shape[2:], BF16)

        @pl.when(z != edge)
        def _():
            remote(
                ch.at[way, d], ch.at[way, d], c_send.at[d], c_recv.at[way, d], sibling
            ).wait_recv()
    arrived(0, 0)
    arrived(1, 3)
    keep = pl.ds(pl.multiple_of(core * shard, shard), shard)
    for b in range(nc):
        total = pj[d, b, keep, :].astype(F32) + ps[d, b].astype(F32)
        total = total + ch[0, d, b].astype(F32) + ch[1, d, b].astype(F32)
        proj_ref[:, b * width:(b + 1) * width] = total.astype(BF16)

    b_out[2].wait_recv()
    b_out[4].wait_recv()
    for b in range(half):
        total = bk[0, b].astype(F32) + rx[0, b].astype(F32) + r2a[b].astype(F32)
        gh_ref[:, b * width:(b + 1) * width] = (total * dsilu[b]).astype(BF16)
    b_out[3].wait_recv()
    b_out[5].wait_recv()
    for b in range(half):
        total = bk[0, half + b].astype(F32) + ry[0, b].astype(F32) + r2b[b].astype(F32)
        gh_ref[:, (half + b) * width:(half + b + 1) * width] = (total * dsilu[half + b]).astype(BF16)

    for copy in a_out + zg_out[1:] + zf_out + ps_out + b_out:
        copy.wait_send()
    for d in range(4):
        @pl.when(group_of[d] != z)
        def _():
            remote(
                psum.at[d], ch.at[0, d], c_send.at[d], c_recv.at[0, d], sibling
            ).wait_send()


def fused_on_device(hidden_pre, weight_blocks, block_rows, block_cols, block_counts, out_grad):
    slots, width = weight_blocks.shape[2], weight_blocks.shape[3]
    group, shard = hidden_pre.shape[0], out_grad.shape[0]
    nb, nc = hidden_pre.shape[1] // width, out_grad.shape[1] // width
    tokens = group * lax.axis_size("col")
    half = nb // 2
    vmem = pl.BlockSpec(memory_space=pltpu.VMEM)
    dma = pltpu.SemaphoreType.DMA
    out = pl.pallas_call(
        fused_kernel,
        out_shape=(
            jax.ShapeDtypeStruct(out_grad.shape, BF16),
            jax.ShapeDtypeStruct(hidden_pre.shape, BF16),
            jax.ShapeDtypeStruct((slots, width, width), F32),
        ),
        in_specs=[pl.BlockSpec(memory_space=pl.ANY)] * 6,
        out_specs=(vmem, vmem, vmem),
        scratch_shapes=[
            pltpu.VMEM(hidden_pre.shape, BF16),
            pltpu.VMEM(weight_blocks.shape, BF16),
            pltpu.SMEM(block_rows.shape, jnp.int32),
            pltpu.SMEM(block_cols.shape, jnp.int32),
            pltpu.SMEM(block_counts.shape, jnp.int32),
            pltpu.VMEM(out_grad.shape, BF16),
            dma((7,)),
            pltpu.VMEM((nb, tokens, width), BF16),
            pltpu.VMEM((nc, tokens, width), BF16),
            pltpu.VMEM((max(nb, nc), group, width), BF16),
            pltpu.VMEM((slots + 1, group, width), F32),
            pltpu.VMEM((nb, group, width), F32),
            pltpu.VMEM((4, nb, group, width), BF16),
            pltpu.VMEM((2, half, group, width), BF16),
            pltpu.VMEM((2, half, group, width), BF16),
            pltpu.VMEM((half, group, width), BF16),
            pltpu.VMEM((half, group, width), BF16),
            pltpu.VMEM((half, group, width), BF16),
            pltpu.VMEM((half, group, width), BF16),
            pltpu.VMEM((4, nc, group, width), BF16),
            pltpu.VMEM((4, nc, shard, width), BF16),
            pltpu.VMEM((4, nc, shard, width), BF16),
            pltpu.VMEM((2, 4, nc, shard, width), BF16),
            pltpu.SMEM((slots,), jnp.int32),
            pltpu.SMEM((nc,), jnp.int32),
            pltpu.SMEM((slots,), jnp.int32),
            pltpu.SMEM((nb,), jnp.int32),
            dma((6,)), dma((6,)), dma((4,)), dma((4,)), dma((4,)), dma((4,)),
            dma((4,)), dma((4,)), dma((4,)), dma((2, 4)), dma((6,)), dma((6,)),
        ],
        compiler_params=pltpu.CompilerParams(
            collective_id=0, has_side_effects=True, vmem_limit_bytes=56 * 1024 * 1024
        ),
    )(
        hidden_pre, weight_blocks, block_rows, block_cols, block_counts, out_grad
    )
    return out[0], out[1], out[2][None, None]


def on_device(hidden_pre, weight_blocks, block_rows, block_cols, block_counts, out_grad):
    fits = (
        lax.axis_size("row") == 8
        and lax.axis_size("col") == 4
        and hidden_pre.shape[0] == 2 * out_grad.shape[0]
        and hidden_pre.shape[1] == out_grad.shape[1]
    )
    body = fused_on_device if fits else plain_on_device
    return body(hidden_pre, weight_blocks, block_rows, block_cols, block_counts, out_grad)


def solution(mesh):
    placed = (
        P("col", "row"),
        P("row", "col", None, None, None),
        P("row", "col", None),
        P("row", "col", None),
        P("row", "col"),
        P("row", "col"),
    )
    return jax.shard_map(
        on_device,
        mesh=mesh,
        in_specs=placed,
        out_specs=(P("row", "col"), P("col", "row"), P("row", "col", None, None, None)),
        check_vma=False,
    )
```

```python
import functools

import jax
import jax.numpy as jnp
from jax import lax
from jax.experimental import pallas as pl
from jax.experimental.pallas import tpu as pltpu
from jax.sharding import PartitionSpec as P

MESH = pl.DeviceIdType.MESH
F32 = jnp.float32
BF16 = jnp.bfloat16


def silu_rounded(values):
    return jax.nn.silu(values.astype(jnp.float32)).astype(jnp.bfloat16)


def pick_blocks(blocks, which):
    return jnp.stack(
        [
            lax.dynamic_index_in_dim(blocks, which[k], axis=1, keepdims=False)
            for k in range(which.shape[0])
        ],
        axis=1,
    )


def plain_on_device(hidden_pre, weight_blocks, block_rows, block_cols, block_counts, out_grad):
    width = weight_blocks.shape[-1]
    slot_count = weight_blocks.shape[2]
    row_span = hidden_pre.shape[1] // width
    col_span = out_grad.shape[1] // width
    row_base = lax.axis_index("row") * row_span
    row_local = block_rows[0, 0] - row_base
    col_local = block_cols[0, 0] - lax.axis_index("col") * col_span
    alive = jnp.arange(slot_count, dtype=jnp.int32) < block_counts[0, 0]
    w_live = jnp.where(
        alive[:, None, None], weight_blocks[0, 0], jnp.zeros_like(weight_blocks[0, 0])
    )
    row_pick = (row_local[:, None] == jnp.arange(row_span, dtype=jnp.int32)[None, :]).astype(
        jnp.float32
    )
    col_pick = (col_local[:, None] == jnp.arange(col_span, dtype=jnp.int32)[None, :]).astype(
        jnp.float32
    )
    grad_full = lax.all_gather(out_grad, "row", axis=0, tiled=True)
    act_rows = silu_rounded(lax.all_gather(hidden_pre, "col", axis=0, tiled=True))
    count = act_rows.shape[0]
    a_stack = pick_blocks(act_rows.reshape(count, row_span, width), row_local)
    prod = jnp.einsum("nkp,kpq->nkq", a_stack, w_live, preferred_element_type=jnp.float32)
    placed = jnp.einsum("nkq,kc->ncq", prod, col_pick, precision=lax.Precision.HIGHEST)
    partial_value = placed.reshape(count, col_span * width)
    grad_rows = grad_full
    act_rows = silu_rounded(lax.all_gather(hidden_pre, "col", axis=0, tiled=True))
    count = act_rows.shape[0]
    a_stack = pick_blocks(act_rows.reshape(count, row_span, width), row_local)
    g_stack = pick_blocks(grad_rows.reshape(count, col_span, width), col_local)
    weight_grad = jnp.einsum("nkp,nkq->kpq", a_stack, g_stack, preferred_element_type=jnp.float32)
    projected = lax.psum_scatter(partial_value, "row", scatter_dimension=0, tiled=True).astype(
        jnp.bfloat16
    )
    count = hidden_pre.shape[0] * lax.axis_size("col")
    grad_rows = grad_full
    g_stack = pick_blocks(grad_rows.reshape(count, col_span, width), col_local)
    back = jnp.einsum("nkq,kpq->nkp", g_stack, w_live, preferred_element_type=jnp.float32)
    placed = jnp.einsum("nkp,kr->nrp", back, row_pick, precision=lax.Precision.HIGHEST)
    back_act = lax.psum_scatter(
        placed.reshape(count, row_span * width), "col", scatter_dimension=0, tiled=True
    )
    hidden_f = hidden_pre.astype(jnp.float32)
    sig = jax.nn.sigmoid(hidden_f)
    grad_hidden = (back_act * (sig * (1.0 + hidden_f * (1.0 - sig)))).astype(jnp.bfloat16)
    grad_blocks = jnp.where(alive[:, None, None], weight_grad, jnp.zeros_like(weight_grad))
    return (projected, grad_hidden, grad_blocks[None, None])


def fused_kernel(
    hidden_hbm, w_hbm, rows_hbm, cols_hbm, count_hbm, grad_hbm,
    proj_ref, gh_ref, gb_ref,
    hidden_ref, w_buf, rows_buf, cols_buf, count_buf, grad_ref, in_sem,
    act_all, g_all, stage, acc, dsilu, bk, rx, ry, r2a, r2b, s2a, s2b,
    pj, ps, psum, ch, prev_c, last_c, prev_r, last_r,
    a_send, a_recv, zg_send, zg_recv, zf_send, zf_recv, ps_send, ps_recv,
    c_send, c_recv, b_send, b_recv,
):
    w_ref, rows_ref, cols_ref = w_buf.at[0, 0], rows_buf.at[0, 0], cols_buf.at[0, 0]
    slots, width = w_buf.shape[2], w_buf.shape[3]
    nb = act_all.shape[0]
    nc = g_all.shape[0]
    half = nb // 2
    split = half * width
    pieces = 4
    piece = nc // pieces
    group = hidden_ref.shape[0]
    shard = grad_ref.shape[0]
    row, col = lax.axis_index("row"), lax.axis_index("col")
    z, core = lax.div(row, 2), lax.rem(row, 2)
    y, x = lax.div(col, 2), lax.rem(col, 2)
    x_peer = {"col": y * 2 + 1 - x}
    y_peer = {"col": (1 - y) * 2 + x}
    sibling = {"row": z * 2 + 1 - core}
    group_of = [
        y * 2 + x,
        y * 2 + 1 - x,
        (1 - y) * 2 + x,
        (1 - y) * 2 + 1 - x,
    ]

    def chip(offset):
        return lax.rem(z + offset, 4)

    def z_peer(offset):
        return {"row": chip(offset) * 2 + core}

    def remote(src, dst, send, recv, to):
        return pltpu.make_async_remote_copy(
            src_ref=src, dst_ref=dst, send_sem=send, recv_sem=recv,
            device_id=to, device_id_type=MESH,
        )

    ins = [
        pltpu.make_async_copy(src, dst, in_sem.at[i])
        for i, (src, dst) in enumerate((
            (hidden_hbm.at[:, pl.ds(0, split)], hidden_ref.at[:, pl.ds(0, split)]),
            (hidden_hbm.at[:, pl.ds(split, split)], hidden_ref.at[:, pl.ds(split, split)]),
            (grad_hbm, grad_ref),
            (rows_hbm, rows_buf),
            (cols_hbm, cols_buf),
            (count_hbm, count_buf),
            (w_hbm, w_buf),
        ))
    ]
    for copy in ins:
        copy.start()
    barrier = pltpu.get_barrier_semaphore()
    for peer in (sibling, x_peer, y_peer, z_peer(1), z_peer(2), z_peer(3)):
        pl.semaphore_signal(barrier, inc=1, device_id=peer, device_id_type=MESH)

    mine = pl.ds(pl.multiple_of(col * group, group), group)
    own_rows = pl.ds(pl.multiple_of(row * shard, shard), shard)

    def activate(blocks):
        for b in blocks:
            v = hidden_ref[:, b * width:(b + 1) * width].astype(F32)
            act_all[b, mine, :] = (v * (1.0 / (1.0 + jnp.exp(-v)))).astype(BF16)

    low, high = pl.ds(0, half), pl.ds(half, half)

    def act_view(part, j):
        return act_all.at[part, pl.ds(pl.multiple_of(j * group, group), group), :]

    def g_view(r):
        return g_all.at[:, pl.ds(pl.multiple_of(r * shard, shard), shard), :]

    def act_copy(i, part, j, to):
        return remote(act_view(part, j), act_view(part, j), a_send.at[i], a_recv.at[i], to)

    a_out = [
        act_copy(0, low, group_of[0], x_peer),
        act_copy(1, high, group_of[0], y_peer),
        act_copy(2, high, group_of[0], x_peer),
        act_copy(3, low, group_of[0], y_peer),
        act_copy(4, low, group_of[1], y_peer),
        act_copy(5, high, group_of[2], x_peer),
    ]
    a_in = [
        act_copy(0, low, group_of[1], x_peer),
        act_copy(1, high, group_of[2], y_peer),
        act_copy(2, high, group_of[1], x_peer),
        act_copy(3, low, group_of[2], y_peer),
        act_copy(4, low, group_of[3], y_peer),
        act_copy(5, high, group_of[3], x_peer),
    ]
    zg_out = [None] + [
        remote(g_view(row), g_view(row), zg_send.at[o], zg_recv.at[o], z_peer(o))
        for o in (1, 2, 3)
    ]
    zg_in, zf_out, zf_in = [], [], []
    for o in range(4):
        got = chip(4 - o) * 2 + core
        other = chip(4 - o) * 2 + 1 - core
        zg_in.append(remote(g_view(got), g_view(got), zg_send.at[o], zg_recv.at[o], z_peer(o)))
        zf_out.append(remote(g_view(got), g_view(got), zf_send.at[o], zf_recv.at[o], sibling))
        zf_in.append(remote(g_view(other), g_view(other), zf_send.at[o], zf_recv.at[o], sibling))

    ins[0].wait()
    activate(range(half))
    pl.semaphore_wait(barrier, 6)
    a_out[0].start()
    a_out[3].start()
    ins[2].wait()
    for b in range(nc):
        g_all[b, own_rows, :] = grad_ref[:, b * width:(b + 1) * width]
    zf_out[0].start()
    for o in (1, 2, 3):
        zg_out[o].start()
    ins[1].wait()
    activate(range(half, nb))
    a_out[1].start()
    a_out[2].start()
    for copy in ins[3:]:
        copy.wait()

    count = count_buf[0, 0]
    row_of = [lax.rem(rows_ref[k], nb) for k in range(slots)]
    col_of = [lax.rem(cols_ref[k], nc) for k in range(slots)]
    for of, prev, last, span in ((col_of, prev_c, last_c, nc), (row_of, prev_r, last_r, nb)):
        for k in range(slots):
            p = jnp.int32(slots)
            for j in range(k):
                p = jnp.where(of[j] == of[k], j, p)
            prev[k] = p
        for b in range(span):
            p = jnp.int32(slots)
            for k in range(slots):
                p = jnp.where((of[k] == b) & (k < count), k, p)
            last[b] = p
    acc[slots] = jnp.zeros(acc.shape[1:], F32)

    def chain(src, slot_of, span, prev, dims):
        def step(k, carry):
            a = stage[lax.rem(slot_of[k], span)]
            prod = lax.dot_general(a, w_ref[k], (dims, ((), ())), preferred_element_type=F32)
            acc[k] = prod + acc[prev[k]]
            return carry
        stage[...] = src
        lax.fori_loop(0, slots, step, 0, unroll=True)

    def rows_of(j):
        return pl.ds(pl.multiple_of(j * group, group), group)

    ps_out = []

    def forward(d):
        chain(act_all[:, rows_of(group_of[d]), :], rows_ref, nb, prev_c, ((1,), (0,)))

        def put(b, carry):
            pj[d, b] = acc[last_c[b]].astype(BF16)
            return carry
        lax.fori_loop(0, nc, put, 0, unroll=True)
        away = pl.ds(pl.multiple_of((1 - core) * shard, shard), shard)
        ps_out.append(remote(pj.at[d, :, away, :], ps.at[d], ps_send.at[d], ps_recv.at[d], sibling))
        ps_out[d].start()

    def advance(d, hop):
        j = group_of[d]
        way = jnp.where(j > z, 0, 1)
        place = jnp.where(j > z, z, 3 - z)
        onward = {"row": (z + 1 - 2 * way) * 2 + core}

        @pl.when((j != z) & (place == hop))
        def _():
            keep = pl.ds(pl.multiple_of(core * shard, shard), shard)
            for c in range(pieces):
                part = pl.ds(c * piece, piece)
                total = pj[d, part, keep, :].astype(F32) + ps[d, part].astype(F32)
                copy = remote(
                    psum.at[d, part], ch.at[way, d, part], c_send.at[d, c],
                    c_recv.at[way, d, c], onward,
                )
                if hop > 0:
                    copy.wait_recv()
                    total = total + ch[way, d, part].astype(F32)
                psum[d, part] = total.astype(BF16)
                copy.start()

    def pair_sum(d):
        ps_out[d].wait_recv()
        advance(d, 0)

    def backward(o):
        j = chip(4 - o)
        chain(g_all[:, rows_of(j), :], cols_ref, nc, prev_r, ((1,), (1,)))
        d = lax.rem(lax.div(j, 2) + y, 2) * 2 + lax.rem(lax.rem(j, 2) + x, 2)

        def put(b, carry):
            bk[d, b] = acc[last_r[b]].astype(BF16)
            return carry
        lax.fori_loop(0, nb, put, 0, unroll=True)

    forward(0)
    zf_in[0].wait_recv()
    backward(0)
    pair_sum(0)
    a_in[0].wait_recv()
    a_out[4].start()
    a_in[1].wait_recv()
    a_out[5].start()
    for b in range(nb):
        v = hidden_ref[:, b * width:(b + 1) * width].astype(F32)
        s = 1.0 / (1.0 + jnp.exp(-v))
        dsilu[b] = s * (1.0 + v * (1.0 - s))
    a_in[2].wait_recv()
    forward(1)
    a_in[3].wait_recv()
    forward(2)
    pair_sum(1)
    pair_sum(2)
    advance(0, 1)
    for o in (1, 2, 3):
        zg_in[o].wait_recv()
        zf_out[o].start()
    for o in (1, 2, 3):
        zf_in[o].wait_recv()
        backward(o)

    b_out = [
        remote(bk.at[3, low], rx.at[1], b_send.at[0], b_recv.at[0], x_peer),
        remote(bk.at[3, high], ry.at[1], b_send.at[1], b_recv.at[1], y_peer),
        remote(bk.at[1, low], rx.at[0], b_send.at[2], b_recv.at[2], x_peer),
        remote(bk.at[2, high], ry.at[0], b_send.at[3], b_recv.at[3], y_peer),
        remote(s2a, r2a, b_send.at[4], b_recv.at[4], y_peer),
        remote(s2b, r2b, b_send.at[5], b_recv.at[5], x_peer),
    ]
    for i in range(4):
        b_out[i].start()
    a_in[4].wait_recv()
    a_in[5].wait_recv()
    forward(3)
    advance(0, 2)
    advance(1, 1)
    advance(2, 1)
    pair_sum(3)
    advance(1, 2)
    advance(2, 2)
    advance(3, 1)
    b_out[0].wait_recv()
    s2a[...] = (bk[2, low].astype(F32) + rx[1].astype(F32)).astype(BF16)
    b_out[4].start()
    b_out[1].wait_recv()
    s2b[...] = (bk[1, high].astype(F32) + ry[1].astype(F32)).astype(BF16)
    b_out[5].start()

    def weight_grad(k, carry):
        a = act_all[lax.rem(rows_ref[k], nb)]
        g = g_all[lax.rem(cols_ref[k], nc)]
        value = lax.dot_general(a, g, (((0,), (0,)), ((), ())), preferred_element_type=F32)
        gb_ref[k] = jnp.where(k < count, value, jnp.zeros_like(value))
        return carry
    lax.fori_loop(0, slots, weight_grad, 0, unroll=True)

    advance(3, 2)
    d = lax.rem(lax.div(z, 2) + y, 2) * 2 + lax.rem(lax.rem(z, 2) + x, 2)

    def arrived(way, edge):
        @pl.when(z == edge)
        def _():
            ch[way, d] = jnp.zeros(ch.shape[2:], BF16)

        @pl.when(z != edge)
        def _():
            for c in range(pieces):
                got = ch.at[way, d, pl.ds(c * piece, piece)]
                remote(got, got, c_send.at[d, c], c_recv.at[way, d, c], sibling).wait_recv()
    arrived(0, 0)
    arrived(1, 3)
    keep = pl.ds(pl.multiple_of(core * shard, shard), shard)
    for b in range(nc):
        total = pj[d, b, keep, :].astype(F32) + ps[d, b].astype(F32)
        total = total + ch[0, d, b].astype(F32) + ch[1, d, b].astype(F32)
        proj_ref[:, b * width:(b + 1) * width] = total.astype(BF16)

    b_out[2].wait_recv()
    b_out[4].wait_recv()
    for b in range(half):
        total = bk[0, b].astype(F32) + rx[0, b].astype(F32) + r2a[b].astype(F32)
        gh_ref[:, b * width:(b + 1) * width] = (total * dsilu[b]).astype(BF16)
    b_out[3].wait_recv()
    b_out[5].wait_recv()
    for b in range(half):
        total = bk[0, half + b].astype(F32) + ry[0, b].astype(F32) + r2b[b].astype(F32)
        gh_ref[:, (half + b) * width:(half + b + 1) * width] = (total * dsilu[half + b]).astype(BF16)

    for copy in a_out + zg_out[1:] + zf_out + ps_out + b_out:
        copy.wait_send()
    for d in range(4):
        @pl.when(group_of[d] != z)
        def _():
            for c in range(pieces):
                part = pl.ds(c * piece, piece)
                remote(
                    psum.at[d, part], ch.at[0, d, part], c_send.at[d, c],
                    c_recv.at[0, d, c], sibling,
                ).wait_send()


def hand_on_kernel(p_in, h_in, b_in, p_out, h_out, b_out, p_buf, h_buf, b_buf, i_sem, o_sem):
    pairs = [(p_in, p_buf, p_out), (h_in, h_buf, h_out)]
    for k in range(b_in.shape[0]):
        pairs.append((b_in.at[k], b_buf.at[k], b_out.at[k]))
    fetches = [
        pltpu.make_async_copy(src, buf, i_sem.at[i]) for i, (src, buf, dst) in enumerate(pairs)
    ]
    stores = [
        pltpu.make_async_copy(buf, dst, o_sem.at[i]) for i, (src, buf, dst) in enumerate(pairs)
    ]
    for fetch in fetches:
        fetch.start()
    for fetch, store in zip(fetches, stores):
        fetch.wait()
        store.start()
    for store in stores:
        store.wait()


def hand_on(proj, grad_hidden, grad_blocks):
    whole = pl.BlockSpec(memory_space=pl.ANY)
    arrays = (proj, grad_hidden, grad_blocks)
    return pl.pallas_call(
        hand_on_kernel,
        out_shape=tuple(jax.ShapeDtypeStruct(a.shape, a.dtype) for a in arrays),
        in_specs=[whole] * 3,
        out_specs=(whole,) * 3,
        scratch_shapes=[pltpu.VMEM(a.shape, a.dtype) for a in arrays]
        + [pltpu.SemaphoreType.DMA((2 + grad_blocks.shape[0],))] * 2,
        compiler_params=pltpu.CompilerParams(vmem_limit_bytes=56 * 1024 * 1024),
    )(*arrays)


def fused_on_device(hidden_pre, weight_blocks, block_rows, block_cols, block_counts, out_grad):
    slots, width = weight_blocks.shape[2], weight_blocks.shape[3]
    group, shard = hidden_pre.shape[0], out_grad.shape[0]
    nb, nc = hidden_pre.shape[1] // width, out_grad.shape[1] // width
    tokens = group * lax.axis_size("col")
    half = nb // 2
    vmem = pl.BlockSpec(memory_space=pltpu.VMEM)
    dma = pltpu.SemaphoreType.DMA
    out = pl.pallas_call(
        fused_kernel,
        out_shape=(
            jax.ShapeDtypeStruct(out_grad.shape, BF16),
            jax.ShapeDtypeStruct(hidden_pre.shape, BF16),
            jax.ShapeDtypeStruct((slots, width, width), F32),
        ),
        in_specs=[pl.BlockSpec(memory_space=pl.ANY)] * 6,
        out_specs=(vmem, vmem, vmem),
        scratch_shapes=[
            pltpu.VMEM(hidden_pre.shape, BF16),
            pltpu.VMEM(weight_blocks.shape, BF16),
            pltpu.SMEM(block_rows.shape, jnp.int32),
            pltpu.SMEM(block_cols.shape, jnp.int32),
            pltpu.SMEM(block_counts.shape, jnp.int32),
            pltpu.VMEM(out_grad.shape, BF16),
            dma((7,)),
            pltpu.VMEM((nb, tokens, width), BF16),
            pltpu.VMEM((nc, tokens, width), BF16),
            pltpu.VMEM((max(nb, nc), group, width), BF16),
            pltpu.VMEM((slots + 1, group, width), F32),
            pltpu.VMEM((nb, group, width), F32),
            pltpu.VMEM((4, nb, group, width), BF16),
            pltpu.VMEM((2, half, group, width), BF16),
            pltpu.VMEM((2, half, group, width), BF16),
            pltpu.VMEM((half, group, width), BF16),
            pltpu.VMEM((half, group, width), BF16),
            pltpu.VMEM((half, group, width), BF16),
            pltpu.VMEM((half, group, width), BF16),
            pltpu.VMEM((4, nc, group, width), BF16),
            pltpu.VMEM((4, nc, shard, width), BF16),
            pltpu.VMEM((4, nc, shard, width), BF16),
            pltpu.VMEM((2, 4, nc, shard, width), BF16),
            pltpu.SMEM((slots,), jnp.int32),
            pltpu.SMEM((nc,), jnp.int32),
            pltpu.SMEM((slots,), jnp.int32),
            pltpu.SMEM((nb,), jnp.int32),
            dma((6,)), dma((6,)), dma((4,)), dma((4,)), dma((4,)), dma((4,)),
            dma((4,)), dma((4,)), dma((4, 4)), dma((2, 4, 4)), dma((6,)), dma((6,)),
        ],
        compiler_params=pltpu.CompilerParams(
            collective_id=0, has_side_effects=True, vmem_limit_bytes=56 * 1024 * 1024
        ),
    )(
        hidden_pre, weight_blocks, block_rows, block_cols, block_counts, out_grad
    )
    outs = hand_on(*out)
    return outs[0], outs[1], outs[2][None, None]


def on_device(hidden_pre, weight_blocks, block_rows, block_cols, block_counts, out_grad):
    fits = (
        lax.axis_size("row") == 8
        and lax.axis_size("col") == 4
        and hidden_pre.shape[0] == 2 * out_grad.shape[0]
        and hidden_pre.shape[1] == out_grad.shape[1]
    )
    body = fused_on_device if fits else plain_on_device
    return body(hidden_pre, weight_blocks, block_rows, block_cols, block_counts, out_grad)


def solution(mesh):
    placed = (
        P("col", "row"),
        P("row", "col", None, None, None),
        P("row", "col", None),
        P("row", "col", None),
        P("row", "col"),
        P("row", "col"),
    )
    return jax.shard_map(
        on_device,
        mesh=mesh,
        in_specs=placed,
        out_specs=(P("row", "col"), P("col", "row"), P("row", "col", None, None, None)),
        check_vma=False,
    )
```

```python
import functools

import jax
import jax.numpy as jnp
from jax import lax
from jax.experimental import pallas as pl
from jax.experimental.pallas import tpu as pltpu
from jax.sharding import PartitionSpec as P

MESH = pl.DeviceIdType.MESH
F32 = jnp.float32
BF16 = jnp.bfloat16


def silu_rounded(values):
    return jax.nn.silu(values.astype(jnp.float32)).astype(jnp.bfloat16)


def pick_blocks(blocks, which):
    return jnp.stack(
        [
            lax.dynamic_index_in_dim(blocks, which[k], axis=1, keepdims=False)
            for k in range(which.shape[0])
        ],
        axis=1,
    )


def plain_on_device(hidden_pre, weight_blocks, block_rows, block_cols, block_counts, out_grad):
    width = weight_blocks.shape[-1]
    slot_count = weight_blocks.shape[2]
    row_span = hidden_pre.shape[1] // width
    col_span = out_grad.shape[1] // width
    row_base = lax.axis_index("row") * row_span
    row_local = block_rows[0, 0] - row_base
    col_local = block_cols[0, 0] - lax.axis_index("col") * col_span
    alive = jnp.arange(slot_count, dtype=jnp.int32) < block_counts[0, 0]
    w_live = jnp.where(
        alive[:, None, None], weight_blocks[0, 0], jnp.zeros_like(weight_blocks[0, 0])
    )
    row_pick = (row_local[:, None] == jnp.arange(row_span, dtype=jnp.int32)[None, :]).astype(
        jnp.float32
    )
    col_pick = (col_local[:, None] == jnp.arange(col_span, dtype=jnp.int32)[None, :]).astype(
        jnp.float32
    )
    grad_full = lax.all_gather(out_grad, "row", axis=0, tiled=True)
    act_rows = silu_rounded(lax.all_gather(hidden_pre, "col", axis=0, tiled=True))
    count = act_rows.shape[0]
    a_stack = pick_blocks(act_rows.reshape(count, row_span, width), row_local)
    prod = jnp.einsum("nkp,kpq->nkq", a_stack, w_live, preferred_element_type=jnp.float32)
    placed = jnp.einsum("nkq,kc->ncq", prod, col_pick, precision=lax.Precision.HIGHEST)
    partial_value = placed.reshape(count, col_span * width)
    grad_rows = grad_full
    act_rows = silu_rounded(lax.all_gather(hidden_pre, "col", axis=0, tiled=True))
    count = act_rows.shape[0]
    a_stack = pick_blocks(act_rows.reshape(count, row_span, width), row_local)
    g_stack = pick_blocks(grad_rows.reshape(count, col_span, width), col_local)
    weight_grad = jnp.einsum("nkp,nkq->kpq", a_stack, g_stack, preferred_element_type=jnp.float32)
    projected = lax.psum_scatter(partial_value, "row", scatter_dimension=0, tiled=True).astype(
        jnp.bfloat16
    )
    count = hidden_pre.shape[0] * lax.axis_size("col")
    grad_rows = grad_full
    g_stack = pick_blocks(grad_rows.reshape(count, col_span, width), col_local)
    back = jnp.einsum("nkq,kpq->nkp", g_stack, w_live, preferred_element_type=jnp.float32)
    placed = jnp.einsum("nkp,kr->nrp", back, row_pick, precision=lax.Precision.HIGHEST)
    back_act = lax.psum_scatter(
        placed.reshape(count, row_span * width), "col", scatter_dimension=0, tiled=True
    )
    hidden_f = hidden_pre.astype(jnp.float32)
    sig = jax.nn.sigmoid(hidden_f)
    grad_hidden = (back_act * (sig * (1.0 + hidden_f * (1.0 - sig)))).astype(jnp.bfloat16)
    grad_blocks = jnp.where(alive[:, None, None], weight_grad, jnp.zeros_like(weight_grad))
    return (projected, grad_hidden, grad_blocks[None, None])


def fused_kernel(
    hidden_hbm, w_hbm, rows_hbm, cols_hbm, count_hbm, grad_hbm,
    proj_ref, gh_ref, gb_ref,
    hidden_ref, w_buf, rows_buf, cols_buf, count_buf, grad_ref, in_sem,
    act_all, g_all, stage, acc, dsilu, bk, rx, ry, r2a, r2b, s2a, s2b,
    pj, ps, psum, ch, prev_c, last_c, prev_r, last_r,
    a_send, a_recv, zg_send, zg_recv, zf_send, zf_recv, ps_send, ps_recv,
    c_send, c_recv, b_send, b_recv,
):
    w_ref, rows_ref, cols_ref = w_buf.at[0, 0], rows_buf.at[0, 0], cols_buf.at[0, 0]
    slots, width = w_buf.shape[2], w_buf.shape[3]
    nb = act_all.shape[0]
    nc = g_all.shape[0]
    half = nb // 2
    split = half * width
    pieces = 8
    piece = nc // pieces
    group = hidden_ref.shape[0]
    shard = grad_ref.shape[0]
    row, col = lax.axis_index("row"), lax.axis_index("col")
    z, core = lax.div(row, 2), lax.rem(row, 2)
    y, x = lax.div(col, 2), lax.rem(col, 2)
    x_peer = {"col": y * 2 + 1 - x}
    y_peer = {"col": (1 - y) * 2 + x}
    sibling = {"row": z * 2 + 1 - core}
    group_of = [
        y * 2 + x,
        y * 2 + 1 - x,
        (1 - y) * 2 + x,
        (1 - y) * 2 + 1 - x,
    ]

    def chip(offset):
        return lax.rem(z + offset, 4)

    def z_peer(offset):
        return {"row": chip(offset) * 2 + core}

    def remote(src, dst, send, recv, to):
        return pltpu.make_async_remote_copy(
            src_ref=src, dst_ref=dst, send_sem=send, recv_sem=recv,
            device_id=to, device_id_type=MESH,
        )

    ins = [
        pltpu.make_async_copy(src, dst, in_sem.at[i])
        for i, (src, dst) in enumerate((
            (hidden_hbm.at[:, pl.ds(0, split)], hidden_ref.at[:, pl.ds(0, split)]),
            (hidden_hbm.at[:, pl.ds(split, split)], hidden_ref.at[:, pl.ds(split, split)]),
            (grad_hbm, grad_ref),
            (rows_hbm, rows_buf),
            (cols_hbm, cols_buf),
            (count_hbm, count_buf),
            (w_hbm, w_buf),
        ))
    ]
    for copy in ins:
        copy.start()
    barrier = pltpu.get_barrier_semaphore()
    for peer in (sibling, x_peer, y_peer, z_peer(1), z_peer(2), z_peer(3)):
        pl.semaphore_signal(barrier, inc=1, device_id=peer, device_id_type=MESH)

    mine = pl.ds(pl.multiple_of(col * group, group), group)
    own_rows = pl.ds(pl.multiple_of(row * shard, shard), shard)

    def activate(blocks):
        for b in blocks:
            v = hidden_ref[:, b * width:(b + 1) * width].astype(F32)
            act_all[b, mine, :] = (v * (1.0 / (1.0 + jnp.exp(-v)))).astype(BF16)

    low, high = pl.ds(0, half), pl.ds(half, half)

    def act_view(part, j):
        return act_all.at[part, pl.ds(pl.multiple_of(j * group, group), group), :]

    def g_view(r):
        return g_all.at[:, pl.ds(pl.multiple_of(r * shard, shard), shard), :]

    def act_copy(i, part, j, to):
        return remote(act_view(part, j), act_view(part, j), a_send.at[i], a_recv.at[i], to)

    a_out = [
        act_copy(0, low, group_of[0], x_peer),
        act_copy(1, high, group_of[0], y_peer),
        act_copy(2, high, group_of[0], x_peer),
        act_copy(3, low, group_of[0], y_peer),
        act_copy(4, low, group_of[1], y_peer),
        act_copy(5, high, group_of[2], x_peer),
    ]
    a_in = [
        act_copy(0, low, group_of[1], x_peer),
        act_copy(1, high, group_of[2], y_peer),
        act_copy(2, high, group_of[1], x_peer),
        act_copy(3, low, group_of[2], y_peer),
        act_copy(4, low, group_of[3], y_peer),
        act_copy(5, high, group_of[3], x_peer),
    ]
    zg_out = [None] + [
        remote(g_view(row), g_view(row), zg_send.at[o], zg_recv.at[o], z_peer(o))
        for o in (1, 2, 3)
    ]
    zg_in, zf_out, zf_in = [], [], []
    for o in range(4):
        got = chip(4 - o) * 2 + core
        other = chip(4 - o) * 2 + 1 - core
        zg_in.append(remote(g_view(got), g_view(got), zg_send.at[o], zg_recv.at[o], z_peer(o)))
        zf_out.append(remote(g_view(got), g_view(got), zf_send.at[o], zf_recv.at[o], sibling))
        zf_in.append(remote(g_view(other), g_view(other), zf_send.at[o], zf_recv.at[o], sibling))

    ins[0].wait()
    activate(range(half))
    pl.semaphore_wait(barrier, 6)
    a_out[0].start()
    a_out[3].start()
    ins[2].wait()
    for b in range(nc):
        g_all[b, own_rows, :] = grad_ref[:, b * width:(b + 1) * width]
    zf_out[0].start()
    for o in (1, 2, 3):
        zg_out[o].start()
    ins[1].wait()
    activate(range(half, nb))
    a_out[1].start()
    a_out[2].start()
    for copy in ins[3:]:
        copy.wait()

    count = count_buf[0, 0]
    row_of = [lax.rem(rows_ref[k], nb) for k in range(slots)]
    col_of = [lax.rem(cols_ref[k], nc) for k in range(slots)]
    for of, prev, last, span in ((col_of, prev_c, last_c, nc), (row_of, prev_r, last_r, nb)):
        for k in range(slots):
            p = jnp.int32(slots)
            for j in range(k):
                p = jnp.where(of[j] == of[k], j, p)
            prev[k] = p
        for b in range(span):
            p = jnp.int32(slots)
            for k in range(slots):
                p = jnp.where((of[k] == b) & (k < count), k, p)
            last[b] = p
    acc[slots] = jnp.zeros(acc.shape[1:], F32)

    def chain(src, slot_of, span, prev, dims):
        def step(k, carry):
            a = stage[lax.rem(slot_of[k], span)]
            prod = lax.dot_general(a, w_ref[k], (dims, ((), ())), preferred_element_type=F32)
            acc[k] = prod + acc[prev[k]]
            return carry
        stage[...] = src
        lax.fori_loop(0, slots, step, 0, unroll=True)

    def rows_of(j):
        return pl.ds(pl.multiple_of(j * group, group), group)

    ps_out = []

    def forward(d):
        chain(act_all[:, rows_of(group_of[d]), :], rows_ref, nb, prev_c, ((1,), (0,)))

        def put(b, carry):
            pj[d, b] = acc[last_c[b]].astype(BF16)
            return carry
        lax.fori_loop(0, nc, put, 0, unroll=True)
        away = pl.ds(pl.multiple_of((1 - core) * shard, shard), shard)
        ps_out.append(remote(pj.at[d, :, away, :], ps.at[d], ps_send.at[d], ps_recv.at[d], sibling))
        ps_out[d].start()

    def advance(d, hop):
        j = group_of[d]
        way = jnp.where(j > z, 0, 1)
        place = jnp.where(j > z, z, 3 - z)
        onward = {"row": (z + 1 - 2 * way) * 2 + core}

        @pl.when((j != z) & (place == hop))
        def _():
            keep = pl.ds(pl.multiple_of(core * shard, shard), shard)
            for c in range(pieces):
                part = pl.ds(c * piece, piece)
                total = pj[d, part, keep, :].astype(F32) + ps[d, part].astype(F32)
                copy = remote(
                    psum.at[d, part], ch.at[way, d, part], c_send.at[d, c],
                    c_recv.at[way, d, c], onward,
                )
                if hop > 0:
                    copy.wait_recv()
                    total = total + ch[way, d, part].astype(F32)
                psum[d, part] = total.astype(BF16)
                copy.start()

    def pair_sum(d):
        ps_out[d].wait_recv()
        advance(d, 0)

    def backward(o):
        j = chip(4 - o)
        chain(g_all[:, rows_of(j), :], cols_ref, nc, prev_r, ((1,), (1,)))
        d = lax.rem(lax.div(j, 2) + y, 2) * 2 + lax.rem(lax.rem(j, 2) + x, 2)

        def put(b, carry):
            bk[d, b] = acc[last_r[b]].astype(BF16)
            return carry
        lax.fori_loop(0, nb, put, 0, unroll=True)

    forward(0)
    zf_in[0].wait_recv()
    backward(0)
    pair_sum(0)
    a_in[0].wait_recv()
    a_out[4].start()
    a_in[1].wait_recv()
    a_out[5].start()
    for b in range(nb):
        v = hidden_ref[:, b * width:(b + 1) * width].astype(F32)
        s = 1.0 / (1.0 + jnp.exp(-v))
        dsilu[b] = s * (1.0 + v * (1.0 - s))
    a_in[2].wait_recv()
    forward(1)
    a_in[3].wait_recv()
    forward(2)
    pair_sum(1)
    pair_sum(2)
    advance(0, 1)
    for o in (1, 2, 3):
        zg_in[o].wait_recv()
        zf_out[o].start()
    for o in (1, 2, 3):
        zf_in[o].wait_recv()
        backward(o)

    b_out = [
        remote(bk.at[3, low], rx.at[1], b_send.at[0], b_recv.at[0], x_peer),
        remote(bk.at[3, high], ry.at[1], b_send.at[1], b_recv.at[1], y_peer),
        remote(bk.at[1, low], rx.at[0], b_send.at[2], b_recv.at[2], x_peer),
        remote(bk.at[2, high], ry.at[0], b_send.at[3], b_recv.at[3], y_peer),
        remote(s2a, r2a, b_send.at[4], b_recv.at[4], y_peer),
        remote(s2b, r2b, b_send.at[5], b_recv.at[5], x_peer),
    ]
    for i in range(4):
        b_out[i].start()
    a_in[4].wait_recv()
    a_in[5].wait_recv()
    forward(3)
    advance(0, 2)
    advance(1, 1)
    advance(2, 1)
    pair_sum(3)
    advance(1, 2)
    advance(2, 2)
    advance(3, 1)
    b_out[0].wait_recv()
    s2a[...] = (bk[2, low].astype(F32) + rx[1].astype(F32)).astype(BF16)
    b_out[4].start()
    b_out[1].wait_recv()
    s2b[...] = (bk[1, high].astype(F32) + ry[1].astype(F32)).astype(BF16)
    b_out[5].start()

    def weight_grad(k, carry):
        a = act_all[lax.rem(rows_ref[k], nb)]
        g = g_all[lax.rem(cols_ref[k], nc)]
        value = lax.dot_general(a, g, (((0,), (0,)), ((), ())), preferred_element_type=F32)
        gb_ref[k] = jnp.where(k < count, value, jnp.zeros_like(value))
        return carry
    lax.fori_loop(0, slots, weight_grad, 0, unroll=True)

    advance(3, 2)
    d = lax.rem(lax.div(z, 2) + y, 2) * 2 + lax.rem(lax.rem(z, 2) + x, 2)

    def arrived(way, edge):
        @pl.when(z == edge)
        def _():
            ch[way, d] = jnp.zeros(ch.shape[2:], BF16)

        @pl.when(z != edge)
        def _():
            for c in range(pieces):
                got = ch.at[way, d, pl.ds(c * piece, piece)]
                remote(got, got, c_send.at[d, c], c_recv.at[way, d, c], sibling).wait_recv()
    arrived(0, 0)
    arrived(1, 3)
    keep = pl.ds(pl.multiple_of(core * shard, shard), shard)
    for b in range(nc):
        total = pj[d, b, keep, :].astype(F32) + ps[d, b].astype(F32)
        total = total + ch[0, d, b].astype(F32) + ch[1, d, b].astype(F32)
        proj_ref[:, b * width:(b + 1) * width] = total.astype(BF16)

    b_out[2].wait_recv()
    b_out[4].wait_recv()
    for b in range(half):
        total = bk[0, b].astype(F32) + rx[0, b].astype(F32) + r2a[b].astype(F32)
        gh_ref[:, b * width:(b + 1) * width] = (total * dsilu[b]).astype(BF16)
    b_out[3].wait_recv()
    b_out[5].wait_recv()
    for b in range(half):
        total = bk[0, half + b].astype(F32) + ry[0, b].astype(F32) + r2b[b].astype(F32)
        gh_ref[:, (half + b) * width:(half + b + 1) * width] = (total * dsilu[half + b]).astype(BF16)

    for copy in a_out + zg_out[1:] + zf_out + ps_out + b_out:
        copy.wait_send()
    for d in range(4):
        @pl.when(group_of[d] != z)
        def _():
            for c in range(pieces):
                part = pl.ds(c * piece, piece)
                remote(
                    psum.at[d, part], ch.at[0, d, part], c_send.at[d, c],
                    c_recv.at[0, d, c], sibling,
                ).wait_send()


def hand_on_kernel(p_in, h_in, b_in, p_out, h_out, b_out, p_buf, h_buf, b_buf, i_sem, o_sem):
    pairs = [(p_in, p_buf, p_out), (h_in, h_buf, h_out)]
    for k in range(b_in.shape[0]):
        pairs.append((b_in.at[k], b_buf.at[k], b_out.at[k]))
    fetches = [
        pltpu.make_async_copy(src, buf, i_sem.at[i]) for i, (src, buf, dst) in enumerate(pairs)
    ]
    stores = [
        pltpu.make_async_copy(buf, dst, o_sem.at[i]) for i, (src, buf, dst) in enumerate(pairs)
    ]
    for fetch in fetches:
        fetch.start()
    for fetch, store in zip(fetches, stores):
        fetch.wait()
        store.start()
    for store in stores:
        store.wait()


def hand_on(proj, grad_hidden, grad_blocks):
    whole = pl.BlockSpec(memory_space=pl.ANY)
    arrays = (proj, grad_hidden, grad_blocks)
    return pl.pallas_call(
        hand_on_kernel,
        out_shape=tuple(jax.ShapeDtypeStruct(a.shape, a.dtype) for a in arrays),
        in_specs=[whole] * 3,
        out_specs=(whole,) * 3,
        scratch_shapes=[pltpu.VMEM(a.shape, a.dtype) for a in arrays]
        + [pltpu.SemaphoreType.DMA((2 + grad_blocks.shape[0],))] * 2,
        compiler_params=pltpu.CompilerParams(vmem_limit_bytes=56 * 1024 * 1024),
    )(*arrays)


def fused_on_device(hidden_pre, weight_blocks, block_rows, block_cols, block_counts, out_grad):
    slots, width = weight_blocks.shape[2], weight_blocks.shape[3]
    group, shard = hidden_pre.shape[0], out_grad.shape[0]
    nb, nc = hidden_pre.shape[1] // width, out_grad.shape[1] // width
    tokens = group * lax.axis_size("col")
    half = nb // 2
    vmem = pl.BlockSpec(memory_space=pltpu.VMEM)
    dma = pltpu.SemaphoreType.DMA
    out = pl.pallas_call(
        fused_kernel,
        out_shape=(
            jax.ShapeDtypeStruct(out_grad.shape, BF16),
            jax.ShapeDtypeStruct(hidden_pre.shape, BF16),
            jax.ShapeDtypeStruct((slots, width, width), F32),
        ),
        in_specs=[pl.BlockSpec(memory_space=pl.ANY)] * 6,
        out_specs=(vmem, vmem, vmem),
        scratch_shapes=[
            pltpu.VMEM(hidden_pre.shape, BF16),
            pltpu.VMEM(weight_blocks.shape, BF16),
            pltpu.SMEM(block_rows.shape, jnp.int32),
            pltpu.SMEM(block_cols.shape, jnp.int32),
            pltpu.SMEM(block_counts.shape, jnp.int32),
            pltpu.VMEM(out_grad.shape, BF16),
            dma((7,)),
            pltpu.VMEM((nb, tokens, width), BF16),
            pltpu.VMEM((nc, tokens, width), BF16),
            pltpu.VMEM((max(nb, nc), group, width), BF16),
            pltpu.VMEM((slots + 1, group, width), F32),
            pltpu.VMEM((nb, group, width), F32),
            pltpu.VMEM((4, nb, group, width), BF16),
            pltpu.VMEM((2, half, group, width), BF16),
            pltpu.VMEM((2, half, group, width), BF16),
            pltpu.VMEM((half, group, width), BF16),
            pltpu.VMEM((half, group, width), BF16),
            pltpu.VMEM((half, group, width), BF16),
            pltpu.VMEM((half, group, width), BF16),
            pltpu.VMEM((4, nc, group, width), BF16),
            pltpu.VMEM((4, nc, shard, width), BF16),
            pltpu.VMEM((4, nc, shard, width), BF16),
            pltpu.VMEM((2, 4, nc, shard, width), BF16),
            pltpu.SMEM((slots,), jnp.int32),
            pltpu.SMEM((nc,), jnp.int32),
            pltpu.SMEM((slots,), jnp.int32),
            pltpu.SMEM((nb,), jnp.int32),
            dma((6,)), dma((6,)), dma((4,)), dma((4,)), dma((4,)), dma((4,)),
            dma((4,)), dma((4,)), dma((4, 8)), dma((2, 4, 8)), dma((6,)), dma((6,)),
        ],
        compiler_params=pltpu.CompilerParams(
            collective_id=0, has_side_effects=True, vmem_limit_bytes=56 * 1024 * 1024
        ),
    )(
        hidden_pre, weight_blocks, block_rows, block_cols, block_counts, out_grad
    )
    outs = hand_on(*out)
    return outs[0], outs[1], outs[2][None, None]


def on_device(hidden_pre, weight_blocks, block_rows, block_cols, block_counts, out_grad):
    fits = (
        lax.axis_size("row") == 8
        and lax.axis_size("col") == 4
        and hidden_pre.shape[0] == 2 * out_grad.shape[0]
        and hidden_pre.shape[1] == out_grad.shape[1]
    )
    body = fused_on_device if fits else plain_on_device
    return body(hidden_pre, weight_blocks, block_rows, block_cols, block_counts, out_grad)


def solution(mesh):
    placed = (
        P("col", "row"),
        P("row", "col", None, None, None),
        P("row", "col", None),
        P("row", "col", None),
        P("row", "col"),
        P("row", "col"),
    )
    return jax.shard_map(
        on_device,
        mesh=mesh,
        in_specs=placed,
        out_specs=(P("row", "col"), P("col", "row"), P("row", "col", None, None, None)),
        check_vma=False,
    )
```
